128 devices in a mesh: doc: 16 (over y, z), feat: 8 (over x, core).
Axes of the slice: x: 4, y: 4, z: 4, core: 2. Of those that a mesh axis runs over, the one named last changes fastest.
Arguments:
- embeddings: bfloat16 [16384, 4096], P('doc'), may hold values from -6 to 6
- projection: bfloat16 [4096, 16384], P(None, 'feat'), may hold values from -0.1875 to 0.1875
- phases: float32 [16384], P('feat'), may hold values from 0 to 6.2831855
- domain_ids: int32 [16384], P('doc'), may hold values from 0 to 511, as said below
- domain_counts: int32 [512], replicated, may hold values from 1 to 2048, as said below
Outputs:
- distances: float32 [512, 512], P('doc')
The draws below stay inside these ranges and needn't reach their ends.
Inputs may be any that keep to these rules, and one draw needn't show every extreme that they name: `domain_ids`: every domain has at least one document. domain_counts[k] is the number of documents whose domain_ids is k.
All inputs are finite; a program needn't handle non-finite values.
Results may differ from the reference program's by a relative error of at most 0.0003.
Values sent between devices are 32-bit elements; how exact they have to be, the bound alone decides.
No kernel may reach another device: no remote copies, remote signals or barrier semaphores. Data moves between devices by JAX's collectives and lax.ppermute only.
A program may use at most 128 MiB of HBM per device.

```python
import math
import jax
import jax.numpy as jnp
from jax import lax

D = 4096
F = 16384
K = 512
DOC_DEV = 1024
DOCS = 16384


def draw_labels(key):
    first, second, third, fourth = jax.random.split(key, 4)
    heavy = DOCS // 8
    left = jax.random.randint(first, (DOCS,), 0, K - 1)
    right = jax.random.randint(second, (DOCS,), 0, K - 1)
    base = jnp.minimum(left, right).astype(jnp.int32)
    order = jax.random.permutation(third, DOCS)
    base = base.at[order[:heavy]].set(jnp.int32(K - 1))
    base = base.at[order[heavy:heavy + K - 1]].set(jnp.arange(K - 1, dtype=jnp.int32))
    relabel = jax.random.permutation(fourth, K).astype(jnp.int32)
    return relabel[base].astype(jnp.int32)


def draw_domain_ids(key, part):
    return draw_labels(key)


def draw_domain_counts(key, part):
    labels = draw_labels(key)
    return jax.ops.segment_sum(jnp.ones((DOCS,), jnp.int32), labels, num_segments=K).astype(jnp.int32)


def steps_of(key, dims, shards, least, top_value):
    def one(axis_at, shards_of):
        steps = jax.random.uniform(jax.random.fold_in(jax.random.fold_in(key, 6), axis_at), (shards_of,), jnp.float32, least / len(shards), top_value / len(shards))
        return jnp.repeat(jnp.exp(steps), dims[axis_at] // shards_of).reshape((-1,) + (1,) * (len(dims) - axis_at - 1))

    gain = one(*shards[0])
    for cut in shards[1:]:
        gain = gain * one(*cut)
    return gain


def bell_draw(own_key, dims, spread, reach, cuts=(), held_as=jnp.bfloat16):
    entries = jax.random.normal(own_key, dims, jnp.float32) * spread
    if len(cuts) > 0:
        entries = steps_of(own_key, dims, cuts, -0.22, 0.18) * entries
    return jnp.clip(entries, min=-reach, max=reach).astype(held_as)


def setup_inputs(seed: int = 0) -> dict:
    streams_of = jax.random.split(jax.random.key(seed), 6)
    embeddings = bell_draw(streams_of[0], (DOCS, D), 1.0, 6.0, ((0, 16),))
    projection = bell_draw(streams_of[1], (D, F), (D // 4) ** -0.5, 0.1875, ((1, 8),))
    phases = jnp.clip(6.2831855 * jax.random.uniform(streams_of[2], (F,), jnp.float32) ** steps_of(streams_of[2], (F,), ((0, 8),), -0.2, 0.2), 0.0, 6.2831855)
    domain_ids = draw_domain_ids(jax.random.fold_in(streams_of[5], 71), 0)
    domain_counts = draw_domain_counts(jax.random.fold_in(streams_of[5], 71), 0)
    return {"embeddings": embeddings, "projection": projection, "phases": phases, "domain_ids": domain_ids, "domain_counts": domain_counts}


def reference(embeddings, projection, phases, domain_ids, domain_counts):
    scale = math.sqrt(2.0 / F)
    blocks = DOCS // DOC_DEV
    emb_blocks = embeddings.reshape(blocks, DOC_DEV, D)
    id_blocks = domain_ids.reshape(blocks, DOC_DEV)

    def add_block(total, item):
        rows, labels = item
        angles = jnp.dot(rows, projection, preferred_element_type=jnp.float32) + phases[None, :]
        features = (scale * jnp.cos(angles)).astype(jnp.bfloat16)
        onehot = (labels[:, None] == jnp.arange(K, dtype=jnp.int32)[None, :]).astype(jnp.bfloat16)
        part = lax.dot_general(onehot, features, (((0,), (0,)), ((), ())), preferred_element_type=jnp.float32)
        return (total + part, None)
    sums, _ = lax.scan(add_block, jnp.zeros((K, F), jnp.float32), (emb_blocks, id_blocks))
    means = sums / domain_counts.astype(jnp.float32)[:, None]
    cross = jnp.dot(means, means.T, precision=lax.Precision.HIGHEST)
    norms = lax.optimization_barrier(jnp.sum(means * means, axis=1))
    return norms[:, None] + norms[None, :] - 2.0 * cross
```

```python
import functools
import math

import jax
import jax.numpy as jnp
from jax import lax
from jax.experimental import pallas as pl
from jax.experimental.pallas import tpu as pltpu
from jax.sharding import PartitionSpec as P

F = 16384
K = 512
RING = 4
LANES = 128
TILE = 256

TWO_PI = 2.0 * math.pi
COS = (0.999999989056354, -19.73920449855692, 64.939117412055, -85.45013861233012, 60.16762307755228, -25.967568454490465, 6.528613369785716)


def scaled_cos(turns):
    r = turns - jnp.round(turns)
    u = r * r
    scale = math.sqrt(2.0 / F)
    value = jnp.float32(scale * COS[-1])
    for c in COS[-2::-1]:
        value = value * u + jnp.float32(scale * c)
    return value


def sums_kernel(n_pieces, where_ref, ids_ref, phase_ref, emb_ref, proj_ref, *rest):
    outs, (angle, onehot) = rest[:n_pieces], rest[n_pieces:]
    piece, half = pl.program_id(0), pl.program_id(1)
    me2 = where_ref[1]
    docs = ids_ref.shape[1]
    last = pl.num_programs(1) - 1

    @pl.when((piece == 0) & (half == 0))
    def _():
        onehot[...] = (
            ids_ref[...] == lax.broadcasted_iota(jnp.int32, (K, docs), 0)
        ).astype(jnp.bfloat16)

    def multiply(slot):
        angle[slot] = jnp.dot(
            emb_ref[slot * TILE : (slot + 1) * TILE, :],
            proj_ref[...],
            preferred_element_type=jnp.float32,
        )

    def collect(out, slot, first_doc, fresh):
        turns = angle[slot] * (1.0 / TWO_PI) + phase_ref[...] * (1.0 / TWO_PI)
        features = scaled_cos(turns).astype(jnp.bfloat16)
        part = jnp.dot(
            onehot[:, pl.ds(first_doc, TILE)], features, preferred_element_type=jnp.float32
        )
        for b in range(RING):
            spot = lax.rem(b - me2 + RING, RING)
            columns = part[:, b * LANES : (b + 1) * LANES]
            out[spot] = columns if fresh else out[spot] + columns

    for p in range(n_pieces):

        @pl.when((piece == p) & (half == 0))
        def _(p=p):
            multiply(0)
            multiply(1)
            collect(outs[p], 0, 0, True)

        @pl.when((piece == p) & (half == last))
        def _(p=p):
            multiply(0)
            collect(outs[p], 1, TILE, False)
            multiply(1)
            collect(outs[p], 0, 2 * TILE, False)
            collect(outs[p], 1, 3 * TILE, False)


def domain_sums(offsets, where, ids, phases, embeddings, projection):
    docs, depth = embeddings.shape
    width = projection.shape[1] // RING
    n = len(offsets)
    step = offsets[1] - offsets[0] if n > 1 else 0

    def column(piece, half, where_ref):
        return (0, lax.rem(where_ref[0] + offsets[0] + piece * step, RING))

    spec = pltpu.PrefetchScalarGridSpec(
        num_scalar_prefetch=1,
        grid=(n, docs // (2 * TILE)),
        in_specs=[
            pl.BlockSpec((1, docs), lambda p, h, w: (0, 0)),
            pl.BlockSpec((1, width), column),
            pl.BlockSpec((2 * TILE, depth), lambda p, h, w: (h, 0)),
            pl.BlockSpec((depth, width), column),
        ],
        out_specs=[pl.BlockSpec((RING, K, LANES), lambda p, h, w: (0, 0, 0))] * n,
        scratch_shapes=[
            pltpu.VMEM((2, TILE, width), jnp.float32),
            pltpu.VMEM((K, docs), jnp.bfloat16),
        ],
    )
    return pl.pallas_call(
        functools.partial(sums_kernel, n),
        grid_spec=spec,
        out_shape=[jax.ShapeDtypeStruct((RING, K, LANES), jnp.float32)] * n,
        compiler_params=pltpu.CompilerParams(vmem_limit_bytes=44 << 20),
        cost_estimate=pl.CostEstimate(
            flops=2 * n * docs * width * (depth + K),
            bytes_accessed=n * (2 * docs * depth + 2 * depth * width + 4 * K * width),
            transcendentals=0,
        ),
        name="domain_sums",
    )(where, ids, phases, embeddings, projection)


def distances_kernel(place_ref, mine_ref, other_ref, *rest):
    outs, (rows,) = rest[:RING], rest[RING:]
    y, z, core = place_ref[0], place_ref[1], place_ref[2]
    part = K // (RING * RING * 2)
    means = jnp.concatenate([mine_ref[...], other_ref[...]], axis=1)
    for s1 in range(RING):
        for s2 in range(RING):
            along_y = lax.rem(y + jnp.where(core == 0, s2, s1), RING)
            along_z = lax.rem(z + jnp.where(core == 0, s1, s2), RING)
            first = pl.multiple_of(((along_y * RING + along_z) * 2 + core) * part, part)
            spot = (s1 * RING + s2) * part
            rows[spot : spot + part, :LANES] = mine_ref[pl.ds(first, part), :]
            rows[spot : spot + part, LANES:] = other_ref[pl.ds(first, part), :]
    picked = rows[...]
    nt = (((1,), (1,)), ((), ()))
    cross = lax.dot_general(
        picked, means, nt, precision=lax.Precision.HIGHEST, preferred_element_type=jnp.float32
    )
    norms = lax.dot_general(
        jnp.ones((8, 2 * LANES), jnp.float32),
        means * means,
        nt,
        precision=lax.Precision.HIGHEST,
        preferred_element_type=jnp.float32,
    )
    own = jnp.sum(picked * picked, axis=1, keepdims=True)
    partial = own + norms[:1, :] - 2.0 * cross
    for s1 in range(RING):
        outs[s1][...] = partial[s1 * RING * part : (s1 + 1) * RING * part].reshape(RING, part, K)


def partial_distances(place, mine, other):
    part = K // (RING * RING * 2)
    return pl.pallas_call(
        distances_kernel,
        out_shape=[jax.ShapeDtypeStruct((RING, part, K), jnp.float32)] * RING,
        in_specs=[
            pl.BlockSpec(memory_space=pltpu.SMEM),
            pl.BlockSpec(memory_space=pltpu.VMEM),
            pl.BlockSpec(memory_space=pltpu.VMEM),
        ],
        out_specs=[pl.BlockSpec(memory_space=pltpu.VMEM)] * RING,
        scratch_shapes=[pltpu.VMEM((K // 2, 2 * LANES), jnp.float32)],
        compiler_params=pltpu.CompilerParams(vmem_limit_bytes=16 << 20),
        name="partial_distances",
    )(place, mine, other)


def device(y, z, x, core):
    return (y % RING * RING + z % RING) * (2 * RING) + x % RING * 2 + core


def everywhere():
    for y in range(RING):
        for z in range(RING):
            for x in range(RING):
                for core in range(2):
                    yield y, z, x, core


def shift(stage, by):
    pairs = []
    for y, z, x, core in everywhere():
        along_z = (core == 0) == (stage == 0)
        target = device(y, z + by, x, core) if along_z else device(y + by, z, x, core)
        pairs.append((device(y, z, x, core), target))
    return pairs


def shift_x(by):
    return [(device(y, z, x, c), device(y, z, x + by, c)) for y, z, x, c in everywhere()]


def swap_core():
    return [(device(y, z, x, c), device(y, z, x, 1 - c)) for y, z, x, c in everywhere()]


def send(value, pairs):
    return lax.ppermute(value, ("doc", "feat"), pairs)


def per_device(embeddings, projection, phases, domain_ids, domain_counts):
    doc, feat = lax.axis_index("doc"), lax.axis_index("feat")
    y, z, core = doc // RING, doc % RING, feat % 2
    me1 = jnp.where(core == 0, z, y)
    me2 = jnp.where(core == 0, y, z)
    where = jnp.stack([me1, me2]).astype(jnp.int32)
    place = jnp.stack([y, z, core]).astype(jnp.int32)
    ids = domain_ids[None, :]
    shifts = phases[None, :]

    (far,) = domain_sums([2], where, ids, shifts, embeddings, projection)
    from_far = send(far, shift(0, 2))
    right, left = domain_sums([1, 3], where, ids, shifts, embeddings, projection)
    from_left = send(right, shift(0, 1))
    from_right = send(left, shift(0, 3))
    (kept,) = domain_sums([0], where, ids, shifts, embeddings, projection)

    blocks = [kept[s] + from_far[s] + from_left[s] + from_right[s] for s in range(RING)]
    sums = blocks[0]
    for s in (2, 1, 3):
        sums = sums + send(blocks[s], shift(1, s))
    means = sums / domain_counts.astype(jnp.float32)[:, None]
    other = send(means, swap_core())

    parts = partial_distances(place, means, other)
    total = parts[0]
    for s in (2, 1, 3):
        total = total + send(parts[s], shift(0, s))
    mine = total[0]
    for s in (2, 1, 3):
        mine = mine + send(total[s], shift(1, s))
    across = [send(mine, shift_x(s)) for s in (2, 1, 3)]
    mine = (mine + across[0]) + (across[1] + across[2])
    theirs = send(mine, swap_core())
    return jnp.where(
        core == 0,
        jnp.concatenate([mine, theirs], axis=0),
        jnp.concatenate([theirs, mine], axis=0),
    )


def solution(mesh):
    in_specs = (P("doc", None), P(None, "feat"), P("feat"), P("doc"), P())
    out_specs = P("doc", None)
    return jax.shard_map(
        per_device, mesh=mesh, in_specs=in_specs, out_specs=out_specs, check_vma=False
    )
```

```python
import functools
import math

import jax
import jax.numpy as jnp
from jax import lax
from jax.experimental import pallas as pl
from jax.experimental.pallas import tpu as pltpu
from jax.sharding import PartitionSpec as P

F = 16384
K = 512
RING = 4
GROUP = K // RING
OWNED = GROUP // RING
DEEP = 4

TWO_PI = 2.0 * math.pi
COS = (0.999999989056354, -19.73920449855692, 64.939117412055, -85.45013861233012, 60.16762307755228, -25.967568454490465, 6.528613369785716)

VMEM = pl.BlockSpec(memory_space=pltpu.VMEM)
SMEM = pl.BlockSpec(memory_space=pltpu.SMEM)
HBM = pl.BlockSpec(memory_space=pltpu.HBM)


def scaled_cos(turns):
    r = turns - jnp.round(turns)
    u = r * r
    scale = math.sqrt(2.0 / F)
    value = jnp.float32(scale * COS[-1])
    for c in COS[-2::-1]:
        value = value * u + jnp.float32(scale * c)
    return value


def span_of(place_ref, piece, width):
    offset, start, size = piece
    first = (place_ref[0] ^ offset) * width + start
    return pl.ds(pl.multiple_of(first, size), size)


def copies_of(place_ref, pieces, width, proj_hbm, into, sems):
    deep = into.shape[0] // DEEP
    copies, at = [], 0
    for piece in pieces:
        columns = span_of(place_ref, piece, width)
        for i in range(DEEP):
            k = pl.ds(i * deep, deep)
            copies.append(
                pltpu.make_async_copy(
                    proj_hbm.at[k, columns], into.at[k, pl.ds(at, piece[2])], sems.at[len(copies)]
                )
            )
        at += piece[2]
    return copies


def phases_of(phase_ref, place_ref, pieces, width):
    parts = [phase_ref[:, span_of(place_ref, piece, width)] for piece in pieces]
    return jnp.concatenate(parts, axis=1) * (1.0 / TWO_PI)


def collect(first, rows, angle, phase, onehot, outs, initial=None):
    span = slice(first, first + rows)
    turns = angle[span] * (1.0 / TWO_PI) + phase
    features = scaled_cos(turns).astype(jnp.bfloat16)
    part = jnp.dot(onehot[:, span], features, preferred_element_type=jnp.float32)
    at = 0
    for out in outs:
        columns = part[:, at : at + out.shape[1]]
        at += out.shape[1]
        if first > 0:
            out[...] += columns
        elif initial is None:
            out[...] = columns
        else:
            out[...] = columns + initial()


def first_kernel(
    offset, after, place_ref, ids_ref, phase_ref, emb_hbm, proj_hbm,
    out_ref, emb_ref, onehot_ref, next_ref,
    proj, angle, sems,
):
    docs, depth = emb_hbm.shape
    width = proj.shape[1]
    half, deep, tile = docs // 2, depth // DEEP, docs // 4
    columns = span_of(place_ref, (offset, 0, width), width)

    copies = []
    for i in range(DEEP):
        k = pl.ds(i * deep, deep)
        copies.append((
            pltpu.make_async_copy(proj_hbm.at[k, columns], proj.at[k], sems.at[2 * i]),
            pltpu.make_async_copy(
                emb_hbm.at[pl.ds(0, half), k], emb_ref.at[pl.ds(0, half), k], sems.at[2 * i + 1]
            ),
        ))
    rest = [
        pltpu.make_async_copy(
            emb_hbm.at[pl.ds(half + i * tile, tile)],
            emb_ref.at[pl.ds(half + i * tile, tile)],
            sems.at[2 * DEEP + i],
        )
        for i in range(2)
    ]
    ahead = copies_of(
        place_ref, after, width, proj_hbm, next_ref, sems.at[pl.ds(2 * DEEP + 2, DEEP * len(after))]
    )
    batches = [list(pair) for pair in copies] + [[copy] for copy in rest] + [ahead]

    def start(i):
        for copy in batches[i]:
            copy.start()

    def wait(i):
        for copy in batches[i]:
            copy.wait()

    always = pl.when(place_ref[0] >= 0)
    for i in range(3):
        start(i)

    @always
    def _():
        row = lax.broadcasted_iota(jnp.int32, (K, 1), 0)
        group = place_ref[1] ^ (row // GROUP)
        inner = row % GROUP
        domain = jnp.where(
            place_ref[2] == 0,
            group * GROUP + inner,
            (inner // OWNED) * GROUP + group * OWNED + inner % OWNED,
        )
        onehot_ref[...] = (ids_ref[...] == domain.astype(jnp.float32)).astype(jnp.bfloat16)

    for i in range(DEEP):
        wait(i)
        start(i + 3)

        @always
        def _(i=i):
            k = slice(i * deep, (i + 1) * deep)
            part = jnp.dot(emb_ref[:half, k], proj[k], preferred_element_type=jnp.float32)
            if i == 0:
                angle[:half] = part
            else:
                angle[:half] += part

    phase = phases_of(phase_ref, place_ref, [(offset, 0, width)], width)
    for i in range(2):
        wait(DEEP + i)

        @always
        def _(i=i):
            span = slice(half + i * tile, half + (i + 1) * tile)
            angle[span] = jnp.dot(emb_ref[span], proj[...], preferred_element_type=jnp.float32)
            if i == 0:
                collect(0, half, angle, phase, onehot_ref, [out_ref])
            else:
                collect(half, tile, angle, phase, onehot_ref, [out_ref])
                collect(half + tile, tile, angle, phase, onehot_ref, [out_ref])

    wait(DEEP + 2)


def next_kernel(
    pieces, after, place_ref, phase_ref, emb_ref, onehot_ref, proj_ref, proj_hbm, *rest
):
    outs, rest = rest[: len(pieces)], rest[len(pieces) :]
    next_ref, angle, sems = rest
    docs, width = emb_ref.shape[0], proj_ref.shape[1]
    tile = docs // 4
    phase = phases_of(phase_ref, place_ref, pieces, width)
    ahead = copies_of(place_ref, after, width, proj_hbm, next_ref, sems)
    for copy in ahead:
        copy.start()

    @pl.when(place_ref[0] >= 0)
    def _():
        for i in range(4):
            span = slice(i * tile, (i + 1) * tile)
            angle[span] = jnp.dot(
                emb_ref[span], proj_ref[...], preferred_element_type=jnp.float32
            )
            if i > 0:
                collect((i - 1) * tile, tile, angle, phase, onehot_ref, outs)
        collect(3 * tile, tile, angle, phase, onehot_ref, outs)

    for copy in ahead:
        copy.wait()


def last_kernel(
    place_ref, phase_ref, emb_ref, onehot_ref, proj_ref, far_ref, left_ref, right_ref, out_ref, angle
):
    docs, width = emb_ref.shape[0], proj_ref.shape[1]
    tile, half = docs // 4, width // 2
    phase = phases_of(phase_ref, place_ref, [(0, 0, width)], width)

    def arrived():
        near = left_ref[...] + right_ref[...]
        return far_ref[...] + jnp.concatenate([near, jnp.zeros_like(near)], axis=1)

    for i in range(4):
        span = slice(i * tile, (i + 1) * tile)
        angle[span] = jnp.dot(emb_ref[span], proj_ref[...], preferred_element_type=jnp.float32)
        if i > 0:
            collect((i - 1) * tile, tile, angle, phase, onehot_ref, [out_ref], arrived)
    collect(3 * tile, tile, angle, phase, onehot_ref, [out_ref], arrived)


def work(docs, depth, width):
    return pl.CostEstimate(
        flops=2 * docs * width * (depth + K),
        bytes_accessed=4 * K * width,
        transcendentals=0,
    )


def first_sums(offset, after, place, ids, phases, embeddings, projection):
    docs, depth = embeddings.shape
    width = projection.shape[1] // RING
    return pl.pallas_call(
        functools.partial(first_kernel, offset, after),
        out_shape=[
            jax.ShapeDtypeStruct((K, width), jnp.float32),
            jax.ShapeDtypeStruct((docs, depth), jnp.bfloat16),
            jax.ShapeDtypeStruct((K, docs), jnp.bfloat16),
            jax.ShapeDtypeStruct((depth, width), jnp.bfloat16),
        ],
        in_specs=[SMEM, VMEM, VMEM, HBM, HBM],
        out_specs=[VMEM] * 4,
        scratch_shapes=[
            pltpu.VMEM((depth, width), jnp.bfloat16),
            pltpu.VMEM((docs, width), jnp.float32),
            pltpu.SemaphoreType.DMA((2 * DEEP + 2 + DEEP * len(after),)),
        ],
        compiler_params=pltpu.CompilerParams(vmem_limit_bytes=32 << 20),
        cost_estimate=work(docs, depth, width),
        name="first_sums",
    )(place, ids, phases, embeddings, projection)


def next_sums(pieces, after, place, phases, emb, onehot, columns, projection):
    docs, depth = emb.shape
    width = columns.shape[1]
    out_shape = [jax.ShapeDtypeStruct((K, size), jnp.float32) for _, _, size in pieces]
    out_shape.append(jax.ShapeDtypeStruct((depth, width), jnp.bfloat16))
    return pl.pallas_call(
        functools.partial(next_kernel, pieces, after),
        out_shape=out_shape,
        in_specs=[SMEM, VMEM, VMEM, VMEM, VMEM, HBM],
        out_specs=[VMEM] * len(out_shape),
        scratch_shapes=[
            pltpu.VMEM((docs, width), jnp.float32),
            pltpu.SemaphoreType.DMA((DEEP * len(after),)),
        ],
        compiler_params=pltpu.CompilerParams(vmem_limit_bytes=24 << 20),
        cost_estimate=work(docs, depth, width),
        name="next_sums",
    )(place, phases, emb, onehot, columns, projection)


def last_sums(place, phases, emb, onehot, columns, far, left, right):
    docs, depth = emb.shape
    width = columns.shape[1]
    return pl.pallas_call(
        last_kernel,
        out_shape=jax.ShapeDtypeStruct((K, width), jnp.float32),
        in_specs=[SMEM] + [VMEM] * 7,
        out_specs=VMEM,
        scratch_shapes=[pltpu.VMEM((docs, width), jnp.float32)],
        compiler_params=pltpu.CompilerParams(vmem_limit_bytes=24 << 20),
        cost_estimate=work(docs, depth, width),
        name="last_sums",
    )(place, phases, emb, onehot, columns, far, left, right)


def distances_kernel(place_ref, *refs):
    groups, outs, (means, rows) = refs[:RING], refs[RING : 2 * RING], refs[2 * RING :]
    me1, me2, core = place_ref[0], place_ref[1], place_ref[2]
    for s in range(RING):
        group = me2 ^ s
        for f in range(RING):
            first = jnp.where(core == 0, group * GROUP + f * OWNED, f * GROUP + group * OWNED)
            first = pl.multiple_of(first, OWNED)
            means[pl.ds(first, OWNED)] = groups[s][f * OWNED : (f + 1) * OWNED]
        owner = pl.multiple_of((me1 ^ s) * OWNED, OWNED)
        rows[s * OWNED : (s + 1) * OWNED] = groups[0][pl.ds(owner, OWNED)]
    nt = (((1,), (1,)), ((), ()))
    every, picked = means[...], rows[...]
    cross = lax.dot_general(
        picked, every, nt, precision=lax.Precision.HIGHEST, preferred_element_type=jnp.float32
    )
    squares = every * every
    lanes = sum(squares[:, i : i + 128] for i in range(0, squares.shape[1], 128))
    norms = jnp.sum(lanes.T, axis=0, keepdims=True)
    own = jnp.sum(picked * picked, axis=1, keepdims=True)
    partial = own + norms - 2.0 * cross
    for s in range(RING):
        outs[s][...] = partial[s * OWNED : (s + 1) * OWNED]


def partial_distances(place, groups):
    width = groups[0].shape[1]
    return pl.pallas_call(
        distances_kernel,
        out_shape=[jax.ShapeDtypeStruct((OWNED, K), jnp.float32)] * RING,
        in_specs=[SMEM] + [VMEM] * RING,
        out_specs=[VMEM] * RING,
        scratch_shapes=[
            pltpu.VMEM((K, width), jnp.float32),
            pltpu.VMEM((GROUP, width), jnp.float32),
        ],
        compiler_params=pltpu.CompilerParams(vmem_limit_bytes=16 << 20),
        name="partial_distances",
    )(place, *groups)


def device(y, z, x, core):
    return (y * RING + z) * (2 * RING) + x * 2 + core


def everywhere():
    for y in range(RING):
        for z in range(RING):
            for x in range(RING):
                for core in range(2):
                    yield y, z, x, core


def across_ring(stage, by):
    pairs = []
    for y, z, x, core in everywhere():
        along_z = (core == 0) == (stage == 0)
        target = device(y, z ^ by, x, core) if along_z else device(y ^ by, z, x, core)
        pairs.append((device(y, z, x, core), target))
    return pairs


def across_x(by):
    return [(device(y, z, x, c), device(y, z, x ^ by, c)) for y, z, x, c in everywhere()]


def across_core():
    return [(device(y, z, x, c), device(y, z, x, 1 - c)) for y, z, x, c in everywhere()]


def send(value, pairs):
    return lax.ppermute(value, ("doc", "feat"), pairs)


def group_counts(domain_counts, me2, core):
    by_y = lax.dynamic_slice_in_dim(domain_counts, me2 * GROUP, GROUP)
    by_z = lax.dynamic_index_in_dim(domain_counts.reshape(RING, RING, OWNED), me2, 1, False)
    return jnp.where(core == 0, by_y, by_z.reshape(GROUP)).astype(jnp.float32)


def per_device(embeddings, projection, phases, domain_ids, domain_counts):
    doc, feat = lax.axis_index("doc"), lax.axis_index("feat")
    y, z, core = doc // RING, doc % RING, feat % 2
    me1 = jnp.where(core == 0, z, y)
    me2 = jnp.where(core == 0, y, z)
    place = jnp.stack([me1, me2, core]).astype(jnp.int32)
    ids = domain_ids.astype(jnp.float32)[None, :]
    phases = phases[None, :]

    width = projection.shape[1] // RING
    half = width // 2
    near = [[(1, at, half), (3, at, half)] for at in (0, half)]
    kept = [(0, 0, width)]
    far, emb, onehot, columns = first_sums(2, near[0], place, ids, phases, embeddings, projection)
    from_far = send(far, across_ring(0, 2))
    right, left, columns = next_sums(
        near[0], near[1], place, phases, emb, onehot, columns, projection
    )
    from_left, from_right = send(right, across_ring(0, 1)), send(left, across_ring(0, 3))
    right, left, columns = next_sums(near[1], kept, place, phases, emb, onehot, columns, projection)
    late = send(right, across_ring(0, 1)), send(left, across_ring(0, 3))
    sums = last_sums(place, phases, emb, onehot, columns, from_far, from_left, from_right)

    sums = jnp.concatenate([sums[:, :half], sums[:, half:] + (late[0] + late[1])], axis=1)
    sums = sums.reshape(RING, GROUP, width)
    mine = sums[0]
    for s in (2, 1, 3):
        mine = mine + send(sums[s], across_ring(1, s))
    mine = mine / group_counts(domain_counts, me2, core)[:, None]
    groups = [mine] + [send(mine, across_ring(1, s)) for s in (1, 2, 3)]

    parts = partial_distances(place, groups)
    total = parts[0]
    for s in (2, 1, 3):
        total = total + send(parts[s], across_ring(0, s))
    across = [send(total, across_x(s)) for s in (2, 1, 3)]
    total = (total + across[0]) + (across[1] + across[2])
    return total + send(total, across_core())


def solution(mesh):
    in_specs = (P("doc", None), P(None, "feat"), P("feat"), P("doc"), P())
    out_specs = P("doc", None)
    return jax.shard_map(
        per_device, mesh=mesh, in_specs=in_specs, out_specs=out_specs, check_vma=False
    )
```

```python
import functools
import math

import jax
import jax.numpy as jnp
from jax import lax
from jax.experimental import pallas as pl
from jax.experimental.pallas import tpu as pltpu
from jax.sharding import PartitionSpec as P

F = 16384
K = 512
RING = 4
LANES = 128
GROUP = K // RING
OWNED = GROUP // RING
DEEP = 4

TWO_PI = 2.0 * math.pi
COS = (0.999999989056354, -19.73920449855692, 64.939117412055, -85.45013861233012, 60.16762307755228, -25.967568454490465, 6.528613369785716)

VMEM = pl.BlockSpec(memory_space=pltpu.VMEM)
SMEM = pl.BlockSpec(memory_space=pltpu.SMEM)
HBM = pl.BlockSpec(memory_space=pltpu.HBM)


def scaled_cos(turns):
    r = turns - jnp.round(turns)
    u = r * r
    scale = math.sqrt(2.0 / F)
    value = jnp.float32(scale * COS[-1])
    for c in COS[-2::-1]:
        value = value * u + jnp.float32(scale * c)
    return value


def span_of(place_ref, piece, width):
    offset, start, size = piece
    first = (place_ref[0] ^ offset) * width + start
    return pl.ds(pl.multiple_of(first, size), size)


def copies_of(place_ref, pieces, width, proj_hbm, into, sems):
    deep = into.shape[0] // DEEP
    copies, at = [], 0
    for piece in pieces:
        columns = span_of(place_ref, piece, width)
        for i in range(DEEP):
            k = pl.ds(i * deep, deep)
            copies.append(
                pltpu.make_async_copy(
                    proj_hbm.at[k, columns], into.at[k, pl.ds(at, piece[2])], sems.at[len(copies)]
                )
            )
        at += piece[2]
    return copies


def phases_of(small_ref, place_ref, pieces, width):
    rows = []
    for offset, start, size in pieces:
        first = ((place_ref[0] ^ offset) * width + start) // LANES
        rows += [small_ref[pl.ds(first + i, 1)] for i in range(size // LANES)]
    return jnp.concatenate(rows, axis=1) * (1.0 / TWO_PI)


def collect(first, rows, angle, phase, onehot, outs, arrived=()):
    span = slice(first, first + rows)
    turns = angle[span] * (1.0 / TWO_PI) + phase
    features = scaled_cos(turns).astype(jnp.bfloat16)
    part = jnp.dot(onehot[:, span], features, preferred_element_type=jnp.float32)
    at = 0
    for i, out in enumerate(outs):
        columns = part[:, at : at + out.shape[1]]
        at += out.shape[1]
        if first > 0:
            out[...] += columns
        elif arrived:
            out[...] = columns + arrived[i][...]
        else:
            out[...] = columns


def first_kernel(
    offset, after, place_ref, small_ref, emb_hbm, proj_hbm,
    low_ref, high_ref, emb_ref, onehot_ref, next_ref,
    proj, angle, sems,
):
    docs, depth = emb_hbm.shape
    width = proj.shape[1]
    half, deep, tile = docs // 2, depth // DEEP, docs // 4
    columns = span_of(place_ref, (offset, 0, width), width)
    outs = [low_ref, high_ref]

    copies, sides = [], (slice(0, half), slice(half, docs))
    for i in range(DEEP):
        k = pl.ds(i * deep, deep)
        copies.append(
            [pltpu.make_async_copy(proj_hbm.at[k, columns], proj.at[k], sems.at[3 * i])]
            + [
                pltpu.make_async_copy(
                    emb_hbm.at[pl.ds(side * half, half), k],
                    emb_ref.at[pl.ds(side * half, half), k],
                    sems.at[3 * i + 1 + side],
                )
                for side in range(2)
            ]
        )
    ahead = copies_of(
        place_ref, after, width, proj_hbm, next_ref, sems.at[pl.ds(3 * DEEP, DEEP * len(after))]
    )
    copies.append(ahead)

    def start(i):
        for copy in copies[i]:
            copy.start()

    for i in range(2):
        start(i)
    row = lax.broadcasted_iota(jnp.int32, (K, 1), 0)
    group = place_ref[1] ^ (row // GROUP)
    inner = row % GROUP
    domain = jnp.where(
        place_ref[2] == 0,
        group * GROUP + inner,
        (inner // OWNED) * GROUP + group * OWNED + inner % OWNED,
    )
    domain = domain.astype(jnp.float32)
    first_row = RING * width // LANES
    for i in range(docs // LANES):
        ids = small_ref[first_row + i : first_row + i + 1]
        onehot_ref[:, i * LANES : (i + 1) * LANES] = (ids == domain).astype(jnp.bfloat16)
    phase = phases_of(small_ref, place_ref, [(offset, 0, width)], width)

    def multiply(i, side):
        k = slice(i * deep, (i + 1) * deep)
        part = jnp.dot(emb_ref[sides[side], k], proj[k], preferred_element_type=jnp.float32)
        if i == 0:
            angle[sides[side]] = part
        else:
            angle[sides[side]] += part

    for i in range(DEEP):
        copies[i][0].wait()
        copies[i][1].wait()
        if i + 2 <= DEEP:
            start(i + 2)
        multiply(i, 0)
        copies[i][2].wait()
        multiply(i, 1)
        if i == DEEP - 1:
            collect(0, half, angle, phase, onehot_ref, outs)
    collect(half, tile, angle, phase, onehot_ref, outs)
    collect(half + tile, tile, angle, phase, onehot_ref, outs)
    for copy in ahead:
        copy.wait()


def next_kernel(
    pieces, after, n_arrived, place_ref, small_ref, emb_ref, onehot_ref, proj_ref, proj_hbm, *rest
):
    arrived, rest = rest[:n_arrived], rest[n_arrived:]
    outs, rest = rest[: len(pieces)], rest[len(pieces) :]
    next_ref, angle, sems = rest
    docs, width = emb_ref.shape[0], proj_ref.shape[1]
    tile = docs // 4
    phase = phases_of(small_ref, place_ref, pieces, width)
    ahead = copies_of(place_ref, after, width, proj_hbm, next_ref, sems)
    for copy in ahead:
        copy.start()

    @pl.when(place_ref[0] >= 0)
    def _():
        for i in range(4):
            span = slice(i * tile, (i + 1) * tile)
            angle[span] = jnp.dot(
                emb_ref[span], proj_ref[...], preferred_element_type=jnp.float32
            )
            if i > 0:
                collect((i - 1) * tile, tile, angle, phase, onehot_ref, outs, arrived)
        collect(3 * tile, tile, angle, phase, onehot_ref, outs)

    for copy in ahead:
        copy.wait()


def last_kernel(
    place_ref, small_ref, emb_ref, onehot_ref, proj_ref, low_ref, high_ref, out_ref, angle
):
    docs, width = emb_ref.shape[0], proj_ref.shape[1]
    tile, half = docs // 4, width // 2
    phase = phases_of(small_ref, place_ref, [(0, 0, width)], width)
    outs = [out_ref.at[:, :half], out_ref.at[:, half:]]
    arrived = [low_ref, high_ref]
    for i in range(4):
        span = slice(i * tile, (i + 1) * tile)
        angle[span] = jnp.dot(emb_ref[span], proj_ref[...], preferred_element_type=jnp.float32)
        if i > 0:
            collect((i - 1) * tile, tile, angle, phase, onehot_ref, outs, arrived)
    collect(3 * tile, tile, angle, phase, onehot_ref, outs)


def work(docs, depth, width):
    return pl.CostEstimate(
        flops=2 * docs * width * (depth + K),
        bytes_accessed=4 * K * width,
        transcendentals=0,
    )


def first_sums(offset, after, place, small, embeddings, projection):
    docs, depth = embeddings.shape
    width = projection.shape[1] // RING
    return pl.pallas_call(
        functools.partial(first_kernel, offset, after),
        out_shape=[
            jax.ShapeDtypeStruct((K, width // 2), jnp.float32),
            jax.ShapeDtypeStruct((K, width // 2), jnp.float32),
            jax.ShapeDtypeStruct((docs, depth), jnp.bfloat16),
            jax.ShapeDtypeStruct((K, docs), jnp.bfloat16),
            jax.ShapeDtypeStruct((depth, width), jnp.bfloat16),
        ],
        in_specs=[SMEM, VMEM, HBM, HBM],
        out_specs=[VMEM] * 5,
        scratch_shapes=[
            pltpu.VMEM((depth, width), jnp.bfloat16),
            pltpu.VMEM((docs, width), jnp.float32),
            pltpu.SemaphoreType.DMA((3 * DEEP + DEEP * len(after),)),
        ],
        compiler_params=pltpu.CompilerParams(vmem_limit_bytes=32 << 20),
        cost_estimate=work(docs, depth, width),
        name="first_sums",
    )(place, small, embeddings, projection)


def next_sums(pieces, after, place, small, emb, onehot, columns, projection, *arrived):
    docs, depth = emb.shape
    width = columns.shape[1]
    out_shape = [jax.ShapeDtypeStruct((K, size), jnp.float32) for _, _, size in pieces]
    out_shape.append(jax.ShapeDtypeStruct((depth, width), jnp.bfloat16))
    return pl.pallas_call(
        functools.partial(next_kernel, pieces, after, len(arrived)),
        out_shape=out_shape,
        in_specs=[SMEM, VMEM, VMEM, VMEM, VMEM, HBM] + [VMEM] * len(arrived),
        out_specs=[VMEM] * len(out_shape),
        scratch_shapes=[
            pltpu.VMEM((docs, width), jnp.float32),
            pltpu.SemaphoreType.DMA((DEEP * len(after),)),
        ],
        compiler_params=pltpu.CompilerParams(vmem_limit_bytes=24 << 20),
        cost_estimate=work(docs, depth, width),
        name="next_sums",
    )(place, small, emb, onehot, columns, projection, *arrived)


def last_sums(place, small, emb, onehot, columns, low, high):
    docs, depth = emb.shape
    width = columns.shape[1]
    return pl.pallas_call(
        last_kernel,
        out_shape=jax.ShapeDtypeStruct((K, width), jnp.float32),
        in_specs=[SMEM] + [VMEM] * 6,
        out_specs=VMEM,
        scratch_shapes=[pltpu.VMEM((docs, width), jnp.float32)],
        compiler_params=pltpu.CompilerParams(vmem_limit_bytes=24 << 20),
        cost_estimate=work(docs, depth, width),
        name="last_sums",
    )(place, small, emb, onehot, columns, low, high)


def distances_kernel(place_ref, *refs):
    groups, outs, (means, rows) = refs[:RING], refs[RING : 2 * RING], refs[2 * RING :]
    me1, me2, core = place_ref[0], place_ref[1], place_ref[2]
    for s in range(RING):
        group = me2 ^ s
        for f in range(RING):
            first = jnp.where(core == 0, group * GROUP + f * OWNED, f * GROUP + group * OWNED)
            first = pl.multiple_of(first, OWNED)
            means[pl.ds(first, OWNED)] = groups[s][f * OWNED : (f + 1) * OWNED]
        owner = pl.multiple_of((me1 ^ s) * OWNED, OWNED)
        rows[s * OWNED : (s + 1) * OWNED] = groups[0][pl.ds(owner, OWNED)]
    nt = (((1,), (1,)), ((), ()))
    every, picked = means[...], rows[...]
    cross = lax.dot_general(
        picked, every, nt, precision=lax.Precision.HIGHEST, preferred_element_type=jnp.float32
    )
    squares = every * every
    lanes = sum(squares[:, i : i + 128] for i in range(0, squares.shape[1], 128))
    norms = jnp.sum(lanes.T, axis=0, keepdims=True)
    own = jnp.sum(picked * picked, axis=1, keepdims=True)
    partial = own + norms - 2.0 * cross
    for s in range(RING):
        outs[s][...] = partial[s * OWNED : (s + 1) * OWNED]


def partial_distances(place, groups):
    width = groups[0].shape[1]
    return pl.pallas_call(
        distances_kernel,
        out_shape=[jax.ShapeDtypeStruct((OWNED, K), jnp.float32)] * RING,
        in_specs=[SMEM] + [VMEM] * RING,
        out_specs=[VMEM] * RING,
        scratch_shapes=[
            pltpu.VMEM((K, width), jnp.float32),
            pltpu.VMEM((GROUP, width), jnp.float32),
        ],
        compiler_params=pltpu.CompilerParams(vmem_limit_bytes=16 << 20),
        name="partial_distances",
    )(place, *groups)


def device(y, z, x, core):
    return (y * RING + z) * (2 * RING) + x * 2 + core


def everywhere():
    for y in range(RING):
        for z in range(RING):
            for x in range(RING):
                for core in range(2):
                    yield y, z, x, core


def across_ring(stage, by):
    pairs = []
    for y, z, x, core in everywhere():
        along_z = (core == 0) == (stage == 0)
        target = device(y, z ^ by, x, core) if along_z else device(y ^ by, z, x, core)
        pairs.append((device(y, z, x, core), target))
    return pairs


def across_x(by):
    return [(device(y, z, x, c), device(y, z, x ^ by, c)) for y, z, x, c in everywhere()]


def across_core():
    return [(device(y, z, x, c), device(y, z, x, 1 - c)) for y, z, x, c in everywhere()]


def send(value, pairs):
    return lax.ppermute(value, ("doc", "feat"), pairs)


def group_counts(domain_counts, me2, core):
    by_y = lax.dynamic_slice_in_dim(domain_counts, me2 * GROUP, GROUP)
    by_z = lax.dynamic_index_in_dim(domain_counts.reshape(RING, RING, OWNED), me2, 1, False)
    return jnp.where(core == 0, by_y, by_z.reshape(GROUP)).astype(jnp.float32)


def per_device(embeddings, projection, phases, domain_ids, domain_counts):
    doc, feat = lax.axis_index("doc"), lax.axis_index("feat")
    y, z, core = doc // RING, doc % RING, feat % 2
    me1 = jnp.where(core == 0, z, y)
    me2 = jnp.where(core == 0, y, z)
    place = jnp.stack([me1, me2, core]).astype(jnp.int32)
    phases, ids = phases.reshape(-1, LANES), domain_ids.reshape(-1, LANES)
    small = jnp.pad(phases, ((0, ids.shape[0]), (0, 0)))
    small = small + jnp.pad(ids, ((phases.shape[0], 0), (0, 0))).astype(jnp.float32)

    width = projection.shape[1] // RING
    half = width // 2
    first = [(1, 0, half), (3, half, half)]
    second = [(3, 0, half), (1, half, half)]
    kept = [(0, 0, width)]
    low, high, emb, onehot, columns = first_sums(
        2, first, place, small, embeddings, projection
    )
    far_low, far_high = send(low, across_ring(0, 1)), send(high, across_ring(0, 3))
    low, high, columns = next_sums(
        first, second, place, small, emb, onehot, columns, projection
    )
    near_low, near_high = send(low, across_ring(0, 1)), send(high, across_ring(0, 3))
    low, high, columns = next_sums(
        second, kept, place, small, emb, onehot, columns, projection, far_low, far_high
    )
    late_low, late_high = send(low, across_ring(0, 3)), send(high, across_ring(0, 1))
    sums = last_sums(place, small, emb, onehot, columns, near_low, near_high)

    sums = jnp.concatenate([sums[:, :half] + late_low, sums[:, half:] + late_high], axis=1)
    sums = sums.reshape(RING, GROUP, width)
    mine = sums[0]
    for s in (2, 1, 3):
        mine = mine + send(sums[s], across_ring(1, s))
    mine = mine / group_counts(domain_counts, me2, core)[:, None]
    groups = [mine] + [send(mine, across_ring(1, s)) for s in (1, 2, 3)]

    parts = partial_distances(place, groups)
    total = parts[0]
    for s in (2, 1, 3):
        total = total + send(parts[s], across_ring(0, s))
    across = [send(total, across_x(s)) for s in (2, 1, 3)]
    total = (total + across[0]) + (across[1] + across[2])
    return total + send(total, across_core())


def solution(mesh):
    in_specs = (P("doc", None), P(None, "feat"), P("feat"), P("doc"), P())
    out_specs = P("doc", None)
    return jax.shard_map(
        per_device, mesh=mesh, in_specs=in_specs, out_specs=out_specs, check_vma=False
    )
```

```python
import functools
import math

import jax
import jax.numpy as jnp
from jax import lax
from jax.experimental import pallas as pl
from jax.experimental.pallas import tpu as pltpu
from jax.sharding import PartitionSpec as P

F = 16384
K = 512
RING = 4
LANES = 128
GROUP = K // RING
OWNED = GROUP // RING
DEEP = 4
CHUNKS = [(0, 512), (512, 512), (1024, 1024), (2048, 1024), (3072, 1024)]

TWO_PI = 2.0 * math.pi
COS = (0.999999989056354, -19.73920449855692, 64.939117412055, -85.45013861233012, 60.16762307755228, -25.967568454490465, 6.528613369785716)

VMEM = pl.BlockSpec(memory_space=pltpu.VMEM)
SMEM = pl.BlockSpec(memory_space=pltpu.SMEM)
HBM = pl.BlockSpec(memory_space=pltpu.HBM)


def scaled_cos(turns):
    r = turns - jnp.round(turns)
    u = r * r
    scale = math.sqrt(2.0 / F)
    value = jnp.float32(scale * COS[-1])
    for c in COS[-2::-1]:
        value = value * u + jnp.float32(scale * c)
    return value


def span_of(place_ref, piece, width):
    offset, side = piece
    half = width // 2
    first = (place_ref[0] ^ offset) * width + ((place_ref[1] // 2) ^ side) * half
    return pl.ds(pl.multiple_of(first, half), half)


def copies_of(place_ref, pieces, width, proj_hbm, into, sems):
    deep = into.shape[0] // DEEP
    copies, at = [], 0
    for piece in pieces:
        columns = span_of(place_ref, piece, width)
        for i in range(DEEP):
            k = pl.ds(i * deep, deep)
            copies.append(
                pltpu.make_async_copy(
                    proj_hbm.at[k, columns], into.at[k, pl.ds(at, width // 2)], sems.at[len(copies)]
                )
            )
        at += width // 2
    return copies


def phases_of(small_ref, place_ref, pieces, width):
    rows, half = [], width // 2
    for offset, side in pieces:
        first = ((place_ref[0] ^ offset) * width + ((place_ref[1] // 2) ^ side) * half) // LANES
        rows += [small_ref[pl.ds(first + i, 1)] for i in range(half // LANES)]
    return jnp.concatenate(rows, axis=1) * (1.0 / TWO_PI)


def collect(first, rows, angle, phase, onehot, outs, arrived=()):
    span = slice(first, first + rows)
    turns = angle[span] * (1.0 / TWO_PI) + phase
    features = scaled_cos(turns).astype(jnp.bfloat16)
    part = jnp.dot(onehot[:, span], features, preferred_element_type=jnp.float32)
    at = 0
    for i, out in enumerate(outs):
        columns = part[:, at : at + out.shape[1]]
        at += out.shape[1]
        if first > 0:
            out[...] += columns
        elif arrived:
            out[...] = columns + arrived[i][...]
        else:
            out[...] = columns


def first_kernel(
    offset, after, place_ref, small_ref, emb_hbm, proj_hbm,
    low_ref, high_ref, emb_ref, onehot_ref, next_ref,
    proj, angle, sems,
):
    docs, depth = emb_hbm.shape
    width = proj.shape[1]
    half, tile = docs // 2, docs // 4
    pieces = [(offset, 0), (offset, 1)]
    outs = [low_ref, high_ref]

    copies, sides = [], (slice(0, half), slice(half, docs))
    for i, (at, size) in enumerate(CHUNKS):
        k = pl.ds(at, size)
        copies.append(
            [
                pltpu.make_async_copy(
                    proj_hbm.at[k, span_of(place_ref, pieces[side], width)],
                    proj.at[k, pl.ds(side * (width // 2), width // 2)],
                    sems.at[4 * i + side],
                )
                for side in range(2)
            ]
            + [
                pltpu.make_async_copy(
                    emb_hbm.at[pl.ds(side * half, half), k],
                    emb_ref.at[pl.ds(side * half, half), k],
                    sems.at[4 * i + 2 + side],
                )
                for side in range(2)
            ]
        )
    ahead = copies_of(
        place_ref, after, width, proj_hbm, next_ref, sems.at[pl.ds(4 * len(CHUNKS), DEEP * len(after))]
    )
    copies.append(ahead)

    def start(i):
        for copy in copies[i]:
            copy.start()

    for i in range(3):
        start(i)
    domain = lax.broadcasted_iota(jnp.int32, (K, 1), 0).astype(jnp.float32)
    first_row = RING * width // LANES
    for i in range(docs // LANES):
        ids = small_ref[first_row + i : first_row + i + 1]
        onehot_ref[:, i * LANES : (i + 1) * LANES] = (ids == domain).astype(jnp.bfloat16)
    phase = phases_of(small_ref, place_ref, pieces, width)

    def multiply(i, side):
        k = slice(CHUNKS[i][0], sum(CHUNKS[i]))
        part = jnp.dot(emb_ref[sides[side], k], proj[k], preferred_element_type=jnp.float32)
        if i == 0:
            angle[sides[side]] = part
        else:
            angle[sides[side]] += part

    for i in range(len(CHUNKS)):
        for copy in copies[i][:3]:
            copy.wait()
        if i + 3 <= len(CHUNKS):
            start(i + 3)
        multiply(i, 0)
        copies[i][3].wait()
        multiply(i, 1)
        if i == len(CHUNKS) - 1:
            collect(0, half, angle, phase, onehot_ref, outs)
    collect(half, tile, angle, phase, onehot_ref, outs)
    collect(half + tile, tile, angle, phase, onehot_ref, outs)
    for copy in ahead:
        copy.wait()


def next_kernel(
    pieces, after, n_arrived, place_ref, small_ref, emb_ref, onehot_ref, proj_ref, proj_hbm, *rest
):
    arrived, rest = rest[:n_arrived], rest[n_arrived:]
    outs, rest = rest[: len(pieces)], rest[len(pieces) :]
    next_ref, angle, sems = rest
    docs, width = emb_ref.shape[0], proj_ref.shape[1]
    tile = docs // 4
    phase = phases_of(small_ref, place_ref, pieces, width)
    ahead = copies_of(place_ref, after, width, proj_hbm, next_ref, sems)
    for copy in ahead:
        copy.start()

    @pl.when(place_ref[0] >= 0)
    def _():
        for i in range(4):
            span = slice(i * tile, (i + 1) * tile)
            angle[span] = jnp.dot(
                emb_ref[span], proj_ref[...], preferred_element_type=jnp.float32
            )
            if i > 0:
                collect((i - 1) * tile, tile, angle, phase, onehot_ref, outs, arrived)
        collect(3 * tile, tile, angle, phase, onehot_ref, outs)

    for copy in ahead:
        copy.wait()


def last_kernel(
    place_ref, small_ref, emb_ref, onehot_ref, proj_ref, low_ref, high_ref, *rest
):
    docs, width = emb_ref.shape[0], proj_ref.shape[1]
    outs, angle = rest[:2], rest[2]
    tile = docs // 4
    phase = phases_of(small_ref, place_ref, [(0, 0), (0, 1)], width)
    arrived = [low_ref, high_ref]
    for i in range(4):
        span = slice(i * tile, (i + 1) * tile)
        angle[span] = jnp.dot(emb_ref[span], proj_ref[...], preferred_element_type=jnp.float32)
        if i > 0:
            collect((i - 1) * tile, tile, angle, phase, onehot_ref, outs, arrived)
    collect(3 * tile, tile, angle, phase, onehot_ref, outs)


def work(docs, depth, width):
    return pl.CostEstimate(
        flops=2 * docs * width * (depth + K),
        bytes_accessed=4 * K * width,
        transcendentals=0,
    )


def first_sums(offset, after, place, small, embeddings, projection):
    docs, depth = embeddings.shape
    width = projection.shape[1] // RING
    return pl.pallas_call(
        functools.partial(first_kernel, offset, after),
        out_shape=[
            jax.ShapeDtypeStruct((K, width // 2), jnp.float32),
            jax.ShapeDtypeStruct((K, width // 2), jnp.float32),
            jax.ShapeDtypeStruct((docs, depth), jnp.bfloat16),
            jax.ShapeDtypeStruct((K, docs), jnp.bfloat16),
            jax.ShapeDtypeStruct((depth, width), jnp.bfloat16),
        ],
        in_specs=[SMEM, VMEM, HBM, HBM],
        out_specs=[VMEM] * 5,
        scratch_shapes=[
            pltpu.VMEM((depth, width), jnp.bfloat16),
            pltpu.VMEM((docs, width), jnp.float32),
            pltpu.SemaphoreType.DMA((4 * len(CHUNKS) + DEEP * len(after),)),
        ],
        compiler_params=pltpu.CompilerParams(vmem_limit_bytes=32 << 20),
        cost_estimate=work(docs, depth, width),
        name="first_sums",
    )(place, small, embeddings, projection)


def next_sums(pieces, after, place, small, emb, onehot, columns, projection, *arrived):
    docs, depth = emb.shape
    width = columns.shape[1]
    out_shape = [jax.ShapeDtypeStruct((K, width // 2), jnp.float32) for _ in pieces]
    out_shape.append(jax.ShapeDtypeStruct((depth, width), jnp.bfloat16))
    return pl.pallas_call(
        functools.partial(next_kernel, pieces, after, len(arrived)),
        out_shape=out_shape,
        in_specs=[SMEM, VMEM, VMEM, VMEM, VMEM, HBM] + [VMEM] * len(arrived),
        out_specs=[VMEM] * len(out_shape),
        scratch_shapes=[
            pltpu.VMEM((docs, width), jnp.float32),
            pltpu.SemaphoreType.DMA((DEEP * len(after),)),
        ],
        compiler_params=pltpu.CompilerParams(vmem_limit_bytes=24 << 20),
        cost_estimate=work(docs, depth, width),
        name="next_sums",
    )(place, small, emb, onehot, columns, projection, *arrived)


def last_sums(place, small, emb, onehot, columns, low, high):
    docs, depth = emb.shape
    width = columns.shape[1]
    return pl.pallas_call(
        last_kernel,
        out_shape=[jax.ShapeDtypeStruct((K, width // 2), jnp.float32)] * 2,
        in_specs=[SMEM] + [VMEM] * 6,
        out_specs=[VMEM] * 2,
        scratch_shapes=[pltpu.VMEM((docs, width), jnp.float32)],
        compiler_params=pltpu.CompilerParams(vmem_limit_bytes=24 << 20),
        cost_estimate=work(docs, depth, width),
        name="last_sums",
    )(place, small, emb, onehot, columns, low, high)


def distances_kernel(place_ref, counts_ref, mine_ref, other_ref, *rest):
    outs, (means, rows, counts) = rest[:RING], rest[RING:]
    y, z, core = place_ref[2], place_ref[3], place_ref[4]
    counts[...] = jnp.broadcast_to(counts_ref[...].astype(jnp.float32), (LANES, K)).T
    means[:, :LANES] = mine_ref[...] / counts[...]
    means[:, LANES:] = other_ref[...] / counts[...]
    part = OWNED // 2
    for s1 in range(RING):
        for s2 in range(RING):
            along_y = y ^ jnp.where(core == 0, s2, s1)
            along_z = z ^ jnp.where(core == 0, s1, s2)
            first = pl.multiple_of(((along_y * RING + along_z) * 2 + core) * part, part)
            spot = (s1 * RING + s2) * part
            rows[spot : spot + part] = means[pl.ds(first, part)]
    nt = (((1,), (1,)), ((), ()))
    every, picked = means[...], rows[...]
    cross = lax.dot_general(
        picked, every, nt, precision=lax.Precision.HIGHEST, preferred_element_type=jnp.float32
    )
    squares = every * every
    norms = jnp.sum((squares[:, :LANES] + squares[:, LANES:]).T, axis=0, keepdims=True)
    own = jnp.sum(picked * picked, axis=1, keepdims=True)
    partial = own + norms - 2.0 * cross
    for s in range(RING):
        outs[s][...] = partial[s * RING * part : (s + 1) * RING * part]


def partial_distances(place, counts, mine, other):
    rows = K // 2
    return pl.pallas_call(
        distances_kernel,
        out_shape=[jax.ShapeDtypeStruct((rows // RING, K), jnp.float32)] * RING,
        in_specs=[SMEM] + [VMEM] * 3,
        out_specs=[VMEM] * RING,
        scratch_shapes=[
            pltpu.VMEM((K, 2 * LANES), jnp.float32),
            pltpu.VMEM((rows, 2 * LANES), jnp.float32),
            pltpu.VMEM((K, LANES), jnp.float32),
        ],
        compiler_params=pltpu.CompilerParams(vmem_limit_bytes=16 << 20),
        name="partial_distances",
    )(place, counts, mine, other)


def device(y, z, x, core):
    return (y * RING + z) * (2 * RING) + x * 2 + core


def everywhere():
    for y in range(RING):
        for z in range(RING):
            for x in range(RING):
                for core in range(2):
                    yield y, z, x, core


def across_ring(stage, by):
    pairs = []
    for y, z, x, core in everywhere():
        along_z = (core == 0) == (stage == 0)
        target = device(y, z ^ by, x, core) if along_z else device(y ^ by, z, x, core)
        pairs.append((device(y, z, x, core), target))
    return pairs


def across_x(by):
    return [(device(y, z, x, c), device(y, z, x ^ by, c)) for y, z, x, c in everywhere()]


def across_core():
    return [(device(y, z, x, c), device(y, z, x, 1 - c)) for y, z, x, c in everywhere()]


def send(value, pairs):
    return lax.ppermute(value, ("doc", "feat"), pairs)


def per_device(embeddings, projection, phases, domain_ids, domain_counts):
    doc, feat = lax.axis_index("doc"), lax.axis_index("feat")
    y, z, core = doc // RING, doc % RING, feat % 2
    me1 = jnp.where(core == 0, z, y)
    me2 = jnp.where(core == 0, y, z)
    place = jnp.stack([me1, me2, y, z, core]).astype(jnp.int32)
    place, odd = lax.optimization_barrier((place, (me2 & 1) == 1))
    phases, ids = phases.reshape(-1, LANES), domain_ids.reshape(-1, LANES)
    small = jnp.pad(phases, ((0, ids.shape[0]), (0, 0)))
    small = small + jnp.pad(ids, ((phases.shape[0], 0), (0, 0))).astype(jnp.float32)

    first, second = [(1, 0), (3, 1)], [(3, 0), (1, 1)]
    kept = [(0, 0), (0, 1)]
    low, high, emb, onehot, columns = first_sums(
        2, first, place, small, embeddings, projection
    )
    far_low, far_high = send(low, across_ring(0, 1)), send(high, across_ring(0, 3))
    low, high, columns = next_sums(
        first, second, place, small, emb, onehot, columns, projection
    )
    near_low, near_high = send(low, across_ring(0, 1)), send(high, across_ring(0, 3))
    low, high, columns = next_sums(
        second, kept, place, small, emb, onehot, columns, projection, far_low, far_high
    )
    late_low, late_high = send(low, across_ring(0, 3)), send(high, across_ring(0, 1))
    low, high = last_sums(place, small, emb, onehot, columns, near_low, near_high)

    low, high = low + late_low, high + late_high
    pieces = []
    for side in (low, high):
        left, right = side[:, :LANES], side[:, LANES:]
        pieces += [jnp.where(odd, right, left), jnp.where(odd, left, right)]
    mine = pieces[0]
    for s in (2, 1, 3):
        mine = mine + send(pieces[s], across_ring(1, s))
    other = send(mine, across_core())

    parts = partial_distances(place, domain_counts[None, :], mine, other)
    total = parts[0]
    for s in (2, 1, 3):
        total = total + send(parts[s], across_ring(0, s))
    total = total.reshape(RING, OWNED // 2, K)
    mine = total[0]
    for s in (2, 1, 3):
        mine = mine + send(total[s], across_ring(1, s))
    near, *far = [send(mine, across_x(s)) for s in (2, 1, 3)]
    mine = (mine + near) + (far[0] + far[1])
    theirs = send(mine, across_core())
    return jnp.where(
        core == 0,
        jnp.concatenate([mine, theirs], axis=0),
        jnp.concatenate([theirs, mine], axis=0),
    )


def solution(mesh):
    in_specs = (P("doc", None), P(None, "feat"), P("feat"), P("doc"), P())
    out_specs = P("doc", None)
    return jax.shard_map(
        per_device, mesh=mesh, in_specs=in_specs, out_specs=out_specs, check_vma=False
    )
```

```python
import functools
import math

import jax
import jax.numpy as jnp
from jax import lax
from jax.experimental import pallas as pl
from jax.experimental.pallas import tpu as pltpu
from jax.sharding import PartitionSpec as P

F = 16384
K = 512
RING = 4
LANES = 128
GROUP = K // RING
OWNED = GROUP // RING
DEEP = 4
CHUNKS = [(0, 512), (512, 512), (1024, 1024), (2048, 1024), (3072, 1024)]

TWO_PI = 2.0 * math.pi
COS = (0.999999989056354, -19.73920449855692, 64.939117412055, -85.45013861233012, 60.16762307755228, -25.967568454490465, 6.528613369785716)

VMEM = pl.BlockSpec(memory_space=pltpu.VMEM)
SMEM = pl.BlockSpec(memory_space=pltpu.SMEM)
HBM = pl.BlockSpec(memory_space=pltpu.HBM)


def scaled_cos(turns):
    r = turns - jnp.round(turns)
    u = r * r
    scale = math.sqrt(2.0 / F)
    value = jnp.float32(scale * COS[-1])
    for c in COS[-2::-1]:
        value = value * u + jnp.float32(scale * c)
    return value


def span_of(place_ref, piece, width):
    offset, side = piece
    half = width // 2
    first = (place_ref[0] ^ offset) * width + ((place_ref[1] // 2) ^ side) * half
    return pl.ds(pl.multiple_of(first, half), half)


def copies_of(place_ref, pieces, width, proj_hbm, into, sems):
    deep = into.shape[0] // DEEP
    copies, at = [], 0
    for piece in pieces:
        columns = span_of(place_ref, piece, width)
        for i in range(DEEP):
            k = pl.ds(i * deep, deep)
            copies.append(
                pltpu.make_async_copy(
                    proj_hbm.at[k, columns], into.at[k, pl.ds(at, width // 2)], sems.at[len(copies)]
                )
            )
        at += width // 2
    return copies


def phases_of(small_ref, place_ref, pieces, width):
    rows, half = [], width // 2
    for offset, side in pieces:
        first = ((place_ref[0] ^ offset) * width + ((place_ref[1] // 2) ^ side) * half) // LANES
        rows += [small_ref[pl.ds(first + i, 1)] for i in range(half // LANES)]
    return jnp.concatenate(rows, axis=1) * (1.0 / TWO_PI)


def collect(first, rows, angle, phase, onehot, outs, arrived=()):
    span = slice(first, first + rows)
    turns = angle[span] * (1.0 / TWO_PI) + phase
    features = scaled_cos(turns).astype(jnp.bfloat16)
    part = jnp.dot(onehot[:, span], features, preferred_element_type=jnp.float32)
    at = 0
    for i, out in enumerate(outs):
        columns = part[:, at : at + out.shape[1]]
        at += out.shape[1]
        if first > 0:
            out[...] += columns
        elif arrived:
            out[...] = columns + arrived[i][...]
        else:
            out[...] = columns


def first_kernel(
    offset, after, place_ref, small_ref, emb_hbm, proj_hbm,
    low_ref, high_ref, emb_ref, onehot_ref, next_ref,
    proj, angle, sems,
):
    docs, depth = emb_hbm.shape
    width = proj.shape[1]
    half, tile = docs // 2, docs // 4
    pieces = [(offset, 0), (offset, 1)]
    outs = [low_ref, high_ref]

    copies, sides = [], (slice(0, half), slice(half, docs))
    for i, (at, size) in enumerate(CHUNKS):
        k = pl.ds(at, size)
        copies.append(
            [
                pltpu.make_async_copy(
                    proj_hbm.at[k, span_of(place_ref, pieces[side], width)],
                    proj.at[k, pl.ds(side * (width // 2), width // 2)],
                    sems.at[4 * i + side],
                )
                for side in range(2)
            ]
            + [
                pltpu.make_async_copy(
                    emb_hbm.at[pl.ds(side * half, half), k],
                    emb_ref.at[pl.ds(side * half, half), k],
                    sems.at[4 * i + 2 + side],
                )
                for side in range(2)
            ]
        )
    ahead = copies_of(
        place_ref, after, width, proj_hbm, next_ref, sems.at[pl.ds(4 * len(CHUNKS), DEEP * len(after))]
    )
    copies.append(ahead)

    def start(i):
        for copy in copies[i]:
            copy.start()

    for i in range(3):
        start(i)
    domain = lax.broadcasted_iota(jnp.int32, (K, 1), 0).astype(jnp.float32)
    first_row = RING * width // LANES
    for i in range(docs // LANES):
        ids = small_ref[first_row + i : first_row + i + 1]
        onehot_ref[:, i * LANES : (i + 1) * LANES] = (ids == domain).astype(jnp.bfloat16)
    phase = phases_of(small_ref, place_ref, pieces, width)

    def multiply(i, side):
        k = slice(CHUNKS[i][0], sum(CHUNKS[i]))
        part = jnp.dot(emb_ref[sides[side], k], proj[k], preferred_element_type=jnp.float32)
        if i == 0:
            angle[sides[side]] = part
        else:
            angle[sides[side]] += part

    for i in range(len(CHUNKS)):
        for copy in copies[i][:3]:
            copy.wait()
        if i + 3 <= len(CHUNKS):
            start(i + 3)
        multiply(i, 0)
        copies[i][3].wait()
        multiply(i, 1)
        if i == len(CHUNKS) - 1:
            collect(0, half, angle, phase, onehot_ref, outs)
    collect(half, tile, angle, phase, onehot_ref, outs)
    collect(half + tile, tile, angle, phase, onehot_ref, outs)
    for copy in ahead:
        copy.wait()


def next_kernel(
    pieces, after, n_arrived, place_ref, small_ref, emb_ref, onehot_ref, proj_ref, proj_hbm, *rest
):
    arrived, rest = rest[:n_arrived], rest[n_arrived:]
    outs, rest = rest[: len(pieces)], rest[len(pieces) :]
    next_ref, angle, sems = rest
    docs, width = emb_ref.shape[0], proj_ref.shape[1]
    tile = docs // 4
    phase = phases_of(small_ref, place_ref, pieces, width)
    ahead = copies_of(place_ref, after, width, proj_hbm, next_ref, sems)
    for copy in ahead:
        copy.start()

    @pl.when(place_ref[0] >= 0)
    def _():
        for i in range(4):
            span = slice(i * tile, (i + 1) * tile)
            angle[span] = jnp.dot(
                emb_ref[span], proj_ref[...], preferred_element_type=jnp.float32
            )
            if i > 0:
                collect((i - 1) * tile, tile, angle, phase, onehot_ref, outs, arrived)
        collect(3 * tile, tile, angle, phase, onehot_ref, outs)

    for copy in ahead:
        copy.wait()


def last_kernel(
    place_ref, small_ref, emb_ref, onehot_ref, proj_ref, low_ref, high_ref, *rest
):
    docs, width = emb_ref.shape[0], proj_ref.shape[1]
    outs, angle = rest[:2], rest[2]
    tile = docs // 4
    phase = phases_of(small_ref, place_ref, [(0, 0), (0, 1)], width)
    arrived = [low_ref, high_ref]
    for i in range(4):
        span = slice(i * tile, (i + 1) * tile)
        angle[span] = jnp.dot(emb_ref[span], proj_ref[...], preferred_element_type=jnp.float32)
        if i > 0:
            collect((i - 1) * tile, tile, angle, phase, onehot_ref, outs, arrived)
    collect(3 * tile, tile, angle, phase, onehot_ref, outs)


def work(docs, depth, width):
    return pl.CostEstimate(
        flops=2 * docs * width * (depth + K),
        bytes_accessed=4 * K * width,
        transcendentals=0,
    )


def first_sums(offset, after, place, small, embeddings, projection):
    docs, depth = embeddings.shape
    width = projection.shape[1] // RING
    return pl.pallas_call(
        functools.partial(first_kernel, offset, after),
        out_shape=[
            jax.ShapeDtypeStruct((K, width // 2), jnp.float32),
            jax.ShapeDtypeStruct((K, width // 2), jnp.float32),
            jax.ShapeDtypeStruct((docs, depth), jnp.bfloat16),
            jax.ShapeDtypeStruct((K, docs), jnp.bfloat16),
            jax.ShapeDtypeStruct((depth, width), jnp.bfloat16),
        ],
        in_specs=[SMEM, VMEM, HBM, HBM],
        out_specs=[VMEM] * 5,
        scratch_shapes=[
            pltpu.VMEM((depth, width), jnp.bfloat16),
            pltpu.VMEM((docs, width), jnp.float32),
            pltpu.SemaphoreType.DMA((4 * len(CHUNKS) + DEEP * len(after),)),
        ],
        compiler_params=pltpu.CompilerParams(vmem_limit_bytes=32 << 20),
        cost_estimate=work(docs, depth, width),
        name="first_sums",
    )(place, small, embeddings, projection)


def next_sums(pieces, after, place, small, emb, onehot, columns, projection, *arrived):
    docs, depth = emb.shape
    width = columns.shape[1]
    out_shape = [jax.ShapeDtypeStruct((K, width // 2), jnp.float32) for _ in pieces]
    out_shape.append(jax.ShapeDtypeStruct((depth, width), jnp.bfloat16))
    return pl.pallas_call(
        functools.partial(next_kernel, pieces, after, len(arrived)),
        out_shape=out_shape,
        in_specs=[SMEM, VMEM, VMEM, VMEM, VMEM, HBM] + [VMEM] * len(arrived),
        out_specs=[VMEM] * len(out_shape),
        scratch_shapes=[
            pltpu.VMEM((docs, width), jnp.float32),
            pltpu.SemaphoreType.DMA((DEEP * len(after),)),
        ],
        compiler_params=pltpu.CompilerParams(vmem_limit_bytes=24 << 20),
        cost_estimate=work(docs, depth, width),
        name="next_sums",
    )(place, small, emb, onehot, columns, projection, *arrived)


def last_sums(place, small, emb, onehot, columns, low, high):
    docs, depth = emb.shape
    width = columns.shape[1]
    return pl.pallas_call(
        last_kernel,
        out_shape=[jax.ShapeDtypeStruct((K, width // 2), jnp.float32)] * 2,
        in_specs=[SMEM] + [VMEM] * 6,
        out_specs=[VMEM] * 2,
        scratch_shapes=[pltpu.VMEM((docs, width), jnp.float32)],
        compiler_params=pltpu.CompilerParams(vmem_limit_bytes=24 << 20),
        cost_estimate=work(docs, depth, width),
        name="last_sums",
    )(place, small, emb, onehot, columns, low, high)


def distances_kernel(place_ref, counts_ref, mine_ref, other_ref, *rest):
    outs, (means, rows, counts) = rest[:RING], rest[RING:]
    y, z, core = place_ref[2], place_ref[3], place_ref[4]
    counts[...] = jnp.broadcast_to(counts_ref[...].astype(jnp.float32), (LANES, K)).T
    means[:, :LANES] = mine_ref[...] / counts[...]
    means[:, LANES:] = other_ref[...] / counts[...]
    part = OWNED // 2
    for s1 in range(RING):
        for s2 in range(RING):
            along_y = y ^ jnp.where(core == 0, s2, s1)
            along_z = z ^ jnp.where(core == 0, s1, s2)
            first = pl.multiple_of(((along_y * RING + along_z) * 2 + core) * part, part)
            spot = (s1 * RING + s2) * part
            rows[spot : spot + part] = means[pl.ds(first, part)]
    nt = (((1,), (1,)), ((), ()))
    every, picked = means[...], rows[...]
    cross = lax.dot_general(
        picked, every, nt, precision=lax.Precision.HIGHEST, preferred_element_type=jnp.float32
    )
    squares = every * every
    norms = jnp.sum((squares[:, :LANES] + squares[:, LANES:]).T, axis=0, keepdims=True)
    own = jnp.sum(picked * picked, axis=1, keepdims=True)
    partial = own + norms - 2.0 * cross
    for s in range(RING):
        outs[s][...] = partial[s * RING * part : (s + 1) * RING * part]


def partial_distances(place, counts, mine, other):
    rows = K // 2
    return pl.pallas_call(
        distances_kernel,
        out_shape=[jax.ShapeDtypeStruct((rows // RING, K), jnp.float32)] * RING,
        in_specs=[SMEM] + [VMEM] * 3,
        out_specs=[VMEM] * RING,
        scratch_shapes=[
            pltpu.VMEM((K, 2 * LANES), jnp.float32),
            pltpu.VMEM((rows, 2 * LANES), jnp.float32),
            pltpu.VMEM((K, LANES), jnp.float32),
        ],
        compiler_params=pltpu.CompilerParams(vmem_limit_bytes=16 << 20),
        name="partial_distances",
    )(place, counts, mine, other)


def device(y, z, x, core):
    return (y * RING + z) * (2 * RING) + x * 2 + core


def everywhere():
    for y in range(RING):
        for z in range(RING):
            for x in range(RING):
                for core in range(2):
                    yield y, z, x, core


def across_ring(stage, by):
    pairs = []
    for y, z, x, core in everywhere():
        along_z = (core == 0) == (stage == 0)
        target = device(y, z ^ by, x, core) if along_z else device(y ^ by, z, x, core)
        pairs.append((device(y, z, x, core), target))
    return pairs


def across_x(by):
    return [(device(y, z, x, c), device(y, z, x ^ by, c)) for y, z, x, c in everywhere()]


def across_core():
    return [(device(y, z, x, c), device(y, z, x, 1 - c)) for y, z, x, c in everywhere()]


def send(value, pairs):
    return lax.ppermute(value, ("doc", "feat"), pairs)


def per_device(embeddings, projection, phases, domain_ids, domain_counts):
    doc, feat = lax.axis_index("doc"), lax.axis_index("feat")
    y, z, core = doc // RING, doc % RING, feat % 2
    me1 = jnp.where(core == 0, z, y)
    me2 = jnp.where(core == 0, y, z)
    place = jnp.stack([me1, me2, y, z, core]).astype(jnp.int32)
    place, odd = lax.optimization_barrier((place, (me2 & 1) == 1))
    phases, ids = phases.reshape(-1, LANES), domain_ids.reshape(-1, LANES)
    small = jnp.pad(phases, ((0, ids.shape[0]), (0, 0)))
    small = small + jnp.pad(ids, ((phases.shape[0], 0), (0, 0))).astype(jnp.float32)

    first, second = [(1, 0), (3, 1)], [(3, 0), (1, 1)]
    kept = [(0, 0), (0, 1)]
    low, high, emb, onehot, columns = first_sums(
        2, first, place, small, embeddings, projection
    )
    far_low, far_high = send(low, across_ring(0, 1)), send(high, across_ring(0, 3))
    low, high, columns = next_sums(
        first, second, place, small, emb, onehot, columns, projection
    )
    near_low, near_high = send(low, across_ring(0, 1)), send(high, across_ring(0, 3))
    low, high, columns = next_sums(
        second, kept, place, small, emb, onehot, columns, projection, far_low, far_high
    )
    late_low, late_high = send(low, across_ring(0, 3)), send(high, across_ring(0, 1))
    low, high = last_sums(place, small, emb, onehot, columns, near_low, near_high)

    low, high = low + late_low, high + late_high
    pieces = []
    for side in (low, high):
        left, right = side[:, :LANES], side[:, LANES:]
        pieces += [jnp.where(odd, right, left), jnp.where(odd, left, right)]
    mine = pieces[0]
    for s in (2, 1, 3):
        mine = mine + send(pieces[s], across_ring(1, s))
    other = send(mine, across_core())

    parts = partial_distances(place, domain_counts[None, :], mine, other)
    total = parts[0]
    for s in (2, 1, 3):
        total = total + send(parts[s], across_ring(0, s))
    total = total.reshape(RING, OWNED // 2, K)
    mine = total[0]
    for s in (2, 1, 3):
        mine = mine + send(total[s], across_ring(1, s))
    first, third, second = [send(mine, across_x(s)) for s in (1, 3, 2)]
    mine = (first + third) + (mine + second)
    theirs = send(mine, across_core())
    return jnp.where(
        core == 0,
        jnp.concatenate([mine, theirs], axis=0),
        jnp.concatenate([theirs, mine], axis=0),
    )


def solution(mesh):
    in_specs = (P("doc", None), P(None, "feat"), P("feat"), P("doc"), P())
    out_specs = P("doc", None)
    return jax.shard_map(
        per_device, mesh=mesh, in_specs=in_specs, out_specs=out_specs, check_vma=False
    )
```

```python
import functools
import math

import jax
import jax.numpy as jnp
from jax import lax
from jax.experimental import pallas as pl
from jax.experimental.pallas import tpu as pltpu
from jax.sharding import PartitionSpec as P

F = 16384
K = 512
RING = 4
LANES = 128
GROUP = K // RING
OWNED = GROUP // RING
DEEP = 4
CHUNKS = [(0, 512), (512, 512), (1024, 1024), (2048, 1024), (3072, 1024)]

TWO_PI = 2.0 * math.pi
COS = (0.999999989056354, -19.73920449855692, 64.939117412055, -85.45013861233012, 60.16762307755228, -25.967568454490465, 6.528613369785716)

VMEM = pl.BlockSpec(memory_space=pltpu.VMEM)
SMEM = pl.BlockSpec(memory_space=pltpu.SMEM)
HBM = pl.BlockSpec(memory_space=pltpu.HBM)


def scaled_cos(turns):
    r = turns - jnp.round(turns)
    u = r * r
    scale = math.sqrt(2.0 / F)
    value = jnp.float32(scale * COS[-1])
    for c in COS[-2::-1]:
        value = value * u + jnp.float32(scale * c)
    return value


def span_of(place_ref, piece, width):
    offset, side = piece
    half = width // 2
    first = (place_ref[0] ^ offset) * width + ((place_ref[1] // 2) ^ side) * half
    return pl.ds(pl.multiple_of(first, half), half)


def copies_of(place_ref, pieces, width, proj_hbm, into, sems):
    deep = into.shape[0] // DEEP
    copies, at = [], 0
    for piece in pieces:
        columns = span_of(place_ref, piece, width)
        for i in range(DEEP):
            k = pl.ds(i * deep, deep)
            copies.append(
                pltpu.make_async_copy(
                    proj_hbm.at[k, columns], into.at[k, pl.ds(at, width // 2)], sems.at[len(copies)]
                )
            )
        at += width // 2
    return copies


def phases_of(small_ref, place_ref, pieces, width):
    rows, half = [], width // 2
    for offset, side in pieces:
        first = ((place_ref[0] ^ offset) * width + ((place_ref[1] // 2) ^ side) * half) // LANES
        rows += [small_ref[pl.ds(first + i, 1)] for i in range(half // LANES)]
    return jnp.concatenate(rows, axis=1) * (1.0 / TWO_PI)


def collect(first, rows, angle, phase, onehot, outs, arrived=()):
    span = slice(first, first + rows)
    turns = angle[span] * (1.0 / TWO_PI) + phase
    features = scaled_cos(turns).astype(jnp.bfloat16)
    part = jnp.dot(onehot[:, span], features, preferred_element_type=jnp.float32)
    at = 0
    for i, out in enumerate(outs):
        columns = part[:, at : at + out.shape[1]]
        at += out.shape[1]
        if first > 0:
            out[...] += columns
        elif arrived:
            out[...] = columns + arrived[i][...]
        else:
            out[...] = columns


def first_kernel(
    offset, after, place_ref, small_ref, emb_hbm, proj_hbm,
    low_ref, high_ref, emb_ref, onehot_ref, next_ref,
    proj, angle, sems,
):
    docs, depth = emb_hbm.shape
    width = proj.shape[1]
    half, tile = docs // 2, docs // 4
    pieces = [(offset, 0), (offset, 1)]
    outs = [low_ref, high_ref]

    copies, sides = [], (slice(0, half), slice(half, docs))
    for i, (at, size) in enumerate(CHUNKS):
        k = pl.ds(at, size)
        copies.append(
            [
                pltpu.make_async_copy(
                    proj_hbm.at[k, span_of(place_ref, pieces[side], width)],
                    proj.at[k, pl.ds(side * (width // 2), width // 2)],
                    sems.at[4 * i + side],
                )
                for side in range(2)
            ]
            + [
                pltpu.make_async_copy(
                    emb_hbm.at[pl.ds(side * half, half), k],
                    emb_ref.at[pl.ds(side * half, half), k],
                    sems.at[4 * i + 2 + side],
                )
                for side in range(2)
            ]
        )
    ahead = copies_of(
        place_ref, after, width, proj_hbm, next_ref, sems.at[pl.ds(4 * len(CHUNKS), DEEP * len(after))]
    )
    copies.append(ahead)

    def start(i):
        for copy in copies[i]:
            copy.start()

    for i in range(3):
        start(i)
    domain = lax.broadcasted_iota(jnp.int32, (K, 1), 0).astype(jnp.float32)
    first_row = RING * width // LANES
    for i in range(docs // LANES):
        ids = small_ref[first_row + i : first_row + i + 1]
        onehot_ref[:, i * LANES : (i + 1) * LANES] = (ids == domain).astype(jnp.bfloat16)
    phase = phases_of(small_ref, place_ref, pieces, width)

    def multiply(i, side):
        k = slice(CHUNKS[i][0], sum(CHUNKS[i]))
        part = jnp.dot(emb_ref[sides[side], k], proj[k], preferred_element_type=jnp.float32)
        if i == 0:
            angle[sides[side]] = part
        else:
            angle[sides[side]] += part

    for i in range(len(CHUNKS)):
        for copy in copies[i][:3]:
            copy.wait()
        if i + 3 <= len(CHUNKS):
            start(i + 3)
        multiply(i, 0)
        copies[i][3].wait()
        multiply(i, 1)
        if i == len(CHUNKS) - 1:
            collect(0, half, angle, phase, onehot_ref, outs)
    collect(half, tile, angle, phase, onehot_ref, outs)
    collect(half + tile, tile, angle, phase, onehot_ref, outs)
    for copy in ahead:
        copy.wait()


def next_kernel(
    pieces, after, n_arrived, place_ref, small_ref, emb_ref, onehot_ref, proj_ref, proj_hbm, *rest
):
    arrived, rest = rest[:n_arrived], rest[n_arrived:]
    outs, rest = rest[: len(pieces)], rest[len(pieces) :]
    next_ref, angle, sems = rest
    docs, width = emb_ref.shape[0], proj_ref.shape[1]
    tile = docs // 4
    phase = phases_of(small_ref, place_ref, pieces, width)
    ahead = copies_of(place_ref, after, width, proj_hbm, next_ref, sems)
    for copy in ahead:
        copy.start()

    @pl.when(place_ref[0] >= 0)
    def _():
        for i in range(4):
            span = slice(i * tile, (i + 1) * tile)
            angle[span] = jnp.dot(
                emb_ref[span], proj_ref[...], preferred_element_type=jnp.float32
            )
            if i > 0:
                collect((i - 1) * tile, tile, angle, phase, onehot_ref, outs, arrived)
        collect(3 * tile, tile, angle, phase, onehot_ref, outs)

    for copy in ahead:
        copy.wait()


def last_kernel(
    place_ref, small_ref, emb_ref, onehot_ref, proj_ref, low_ref, high_ref, *rest
):
    docs, width = emb_ref.shape[0], proj_ref.shape[1]
    outs, angle = rest[:2], rest[2]
    tile = docs // 4
    phase = phases_of(small_ref, place_ref, [(0, 0), (0, 1)], width)
    arrived = [low_ref, high_ref]
    for i in range(4):
        span = slice(i * tile, (i + 1) * tile)
        angle[span] = jnp.dot(emb_ref[span], proj_ref[...], preferred_element_type=jnp.float32)
        if i > 0:
            collect((i - 1) * tile, tile, angle, phase, onehot_ref, outs, arrived)
    collect(3 * tile, tile, angle, phase, onehot_ref, outs)


def work(docs, depth, width):
    return pl.CostEstimate(
        flops=2 * docs * width * (depth + K),
        bytes_accessed=4 * K * width,
        transcendentals=0,
    )


def first_sums(offset, after, place, small, embeddings, projection):
    docs, depth = embeddings.shape
    width = projection.shape[1] // RING
    return pl.pallas_call(
        functools.partial(first_kernel, offset, after),
        out_shape=[
            jax.ShapeDtypeStruct((K, width // 2), jnp.float32),
            jax.ShapeDtypeStruct((K, width // 2), jnp.float32),
            jax.ShapeDtypeStruct((docs, depth), jnp.bfloat16),
            jax.ShapeDtypeStruct((K, docs), jnp.bfloat16),
            jax.ShapeDtypeStruct((depth, width), jnp.bfloat16),
        ],
        in_specs=[SMEM, VMEM, HBM, HBM],
        out_specs=[VMEM] * 5,
        scratch_shapes=[
            pltpu.VMEM((depth, width), jnp.bfloat16),
            pltpu.VMEM((docs, width), jnp.float32),
            pltpu.SemaphoreType.DMA((4 * len(CHUNKS) + DEEP * len(after),)),
        ],
        compiler_params=pltpu.CompilerParams(vmem_limit_bytes=32 << 20),
        cost_estimate=work(docs, depth, width),
        name="first_sums",
    )(place, small, embeddings, projection)


def next_sums(pieces, after, place, small, emb, onehot, columns, projection, *arrived):
    docs, depth = emb.shape
    width = columns.shape[1]
    out_shape = [jax.ShapeDtypeStruct((K, width // 2), jnp.float32) for _ in pieces]
    out_shape.append(jax.ShapeDtypeStruct((depth, width), jnp.bfloat16))
    return pl.pallas_call(
        functools.partial(next_kernel, pieces, after, len(arrived)),
        out_shape=out_shape,
        in_specs=[SMEM, VMEM, VMEM, VMEM, VMEM, HBM] + [VMEM] * len(arrived),
        out_specs=[VMEM] * len(out_shape),
        scratch_shapes=[
            pltpu.VMEM((docs, width), jnp.float32),
            pltpu.SemaphoreType.DMA((DEEP * len(after),)),
        ],
        compiler_params=pltpu.CompilerParams(vmem_limit_bytes=24 << 20),
        cost_estimate=work(docs, depth, width),
        name="next_sums",
    )(place, small, emb, onehot, columns, projection, *arrived)


def last_sums(place, small, emb, onehot, columns, low, high):
    docs, depth = emb.shape
    width = columns.shape[1]
    return pl.pallas_call(
        last_kernel,
        out_shape=[jax.ShapeDtypeStruct((K, width // 2), jnp.float32)] * 2,
        in_specs=[SMEM] + [VMEM] * 6,
        out_specs=[VMEM] * 2,
        scratch_shapes=[pltpu.VMEM((docs, width), jnp.float32)],
        compiler_params=pltpu.CompilerParams(vmem_limit_bytes=24 << 20),
        cost_estimate=work(docs, depth, width),
        name="last_sums",
    )(place, small, emb, onehot, columns, low, high)


def distances_kernel(n_before, place_ref, counts_ref, sums_ref, *rest):
    before, rest = rest[:n_before], rest[n_before:]
    outs, (means, rows, counts) = rest[:RING], rest[RING:]
    y, z, core = place_ref[2], place_ref[3], place_ref[4]
    counts[...] = jnp.broadcast_to(counts_ref[...].astype(jnp.float32), (LANES, K)).T
    means[...] = sums_ref[...] / counts[...]
    part = OWNED // 2
    for s1 in range(RING):
        for s2 in range(RING):
            along_y = y ^ jnp.where(core == 0, s2, s1)
            along_z = z ^ jnp.where(core == 0, s1, s2)
            first = pl.multiple_of(((along_y * RING + along_z) * 2 + core) * part, part)
            spot = (s1 * RING + s2) * part
            rows[spot : spot + part] = means[pl.ds(first, part)]
    nt = (((1,), (1,)), ((), ()))
    every, picked = means[...], rows[...]
    cross = lax.dot_general(
        picked, every, nt, precision=lax.Precision.HIGHEST, preferred_element_type=jnp.float32
    )
    squares = every * every
    norms = jnp.sum(squares.T, axis=0, keepdims=True)
    own = jnp.sum(picked * picked, axis=1, keepdims=True)
    partial = own + norms - 2.0 * cross
    for s in range(RING):
        block = partial[s * RING * part : (s + 1) * RING * part]
        outs[s][...] = before[s][...] + block if before else block


def partial_distances(place, counts, sums, *before):
    rows = K // 2
    return pl.pallas_call(
        functools.partial(distances_kernel, len(before)),
        out_shape=[jax.ShapeDtypeStruct((rows // RING, K), jnp.float32)] * RING,
        in_specs=[SMEM] + [VMEM] * (2 + len(before)),
        out_specs=[VMEM] * RING,
        scratch_shapes=[
            pltpu.VMEM((K, LANES), jnp.float32),
            pltpu.VMEM((rows, LANES), jnp.float32),
            pltpu.VMEM((K, LANES), jnp.float32),
        ],
        compiler_params=pltpu.CompilerParams(vmem_limit_bytes=16 << 20),
        name="partial_distances",
    )(place, counts, sums, *before)


def device(y, z, x, core):
    return (y * RING + z) * (2 * RING) + x * 2 + core


def everywhere():
    for y in range(RING):
        for z in range(RING):
            for x in range(RING):
                for core in range(2):
                    yield y, z, x, core


def across_ring(stage, by):
    pairs = []
    for y, z, x, core in everywhere():
        along_z = (core == 0) == (stage == 0)
        target = device(y, z ^ by, x, core) if along_z else device(y ^ by, z, x, core)
        pairs.append((device(y, z, x, core), target))
    return pairs


def across_x(by):
    return [(device(y, z, x, c), device(y, z, x ^ by, c)) for y, z, x, c in everywhere()]


def across_core():
    return [(device(y, z, x, c), device(y, z, x, 1 - c)) for y, z, x, c in everywhere()]


def send(value, pairs):
    return lax.ppermute(value, ("doc", "feat"), pairs)


def per_device(embeddings, projection, phases, domain_ids, domain_counts):
    doc, feat = lax.axis_index("doc"), lax.axis_index("feat")
    y, z, core = doc // RING, doc % RING, feat % 2
    me1 = jnp.where(core == 0, z, y)
    me2 = jnp.where(core == 0, y, z)
    place = jnp.stack([me1, me2, y, z, core]).astype(jnp.int32)
    place, odd = lax.optimization_barrier((place, (me2 & 1) == 1))
    phases, ids = phases.reshape(-1, LANES), domain_ids.reshape(-1, LANES)
    small = jnp.pad(phases, ((0, ids.shape[0]), (0, 0)))
    small = small + jnp.pad(ids, ((phases.shape[0], 0), (0, 0))).astype(jnp.float32)

    first, second = [(1, 0), (3, 1)], [(3, 0), (1, 1)]
    kept = [(0, 0), (0, 1)]
    low, high, emb, onehot, columns = first_sums(
        2, first, place, small, embeddings, projection
    )
    far_low, far_high = send(low, across_ring(0, 1)), send(high, across_ring(0, 3))
    low, high, columns = next_sums(
        first, second, place, small, emb, onehot, columns, projection
    )
    near_low, near_high = send(low, across_ring(0, 1)), send(high, across_ring(0, 3))
    low, high, columns = next_sums(
        second, kept, place, small, emb, onehot, columns, projection, far_low, far_high
    )
    late_low, late_high = send(low, across_ring(0, 3)), send(high, across_ring(0, 1))
    low, high = last_sums(place, small, emb, onehot, columns, near_low, near_high)

    low, high = low + late_low, high + late_high
    pieces = []
    for side in (low, high):
        left, right = side[:, :LANES], side[:, LANES:]
        pieces += [jnp.where(odd, right, left), jnp.where(odd, left, right)]
    mine = pieces[0]
    for s in (2, 1, 3):
        mine = mine + send(pieces[s], across_ring(1, s))
    other = send(mine, across_core())

    counts = domain_counts[None, :]
    parts = partial_distances(place, counts, mine)
    parts = partial_distances(place, counts, other, *parts)
    total = parts[0]
    for s in (2, 1, 3):
        total = total + send(parts[s], across_ring(0, s))
    total = total.reshape(RING, OWNED // 2, K)
    mine = total[0]
    for s in (2, 1, 3):
        mine = mine + send(total[s], across_ring(1, s))
    first, third, second = [send(mine, across_x(s)) for s in (1, 3, 2)]
    mine = (first + third) + (mine + second)
    theirs = send(mine, across_core())
    return jnp.where(
        core == 0,
        jnp.concatenate([mine, theirs], axis=0),
        jnp.concatenate([theirs, mine], axis=0),
    )


def solution(mesh):
    in_specs = (P("doc", None), P(None, "feat"), P("feat"), P("doc"), P())
    out_specs = P("doc", None)
    return jax.shard_map(
        per_device, mesh=mesh, in_specs=in_specs, out_specs=out_specs, check_vma=False
    )
```
